32 devices in a mesh: req: 8 (over y, x, core), head: 4 (over z).
Axes of the slice: x: 2, y: 2, z: 4, core: 2. Of those that a mesh axis runs over, the one named last changes fastest.
Arguments:
- hidden: bfloat16 [256, 16, 2048], P('req', None, 'head'), may hold values from -6 to 6
- w_zx: bfloat16 [2048, 2, 4096], P(None, None, 'head'), may hold values from -0.125 to 0.125
- w_bc: bfloat16 [2048, 256], replicated, may hold values from -0.125 to 0.125
- w_dt: bfloat16 [2048, 64], P(None, 'head'), may hold values from -0.125 to 0.125
- conv_x_w: float32 [5, 4096], P(None, 'head'), may hold values from -3 to 3
- conv_bc_w: float32 [5, 256], replicated, may hold values from -3 to 3
- dt_bias: float32 [64], P('head'), may hold values from -4 to 0.5
- a_log: float32 [64], P('head'), may hold values from 0 to 2.5
- d_skip: float32 [64], P('head'), may hold values from 0.5 to 1.5
- norm_gain: float32 [4096], P('head'), may hold values from 0.1 to 1.9
- w_out: bfloat16 [4096, 2048], P('head'), may hold values from -0.09375 to 0.09375
- ssm_state: float32 [256, 64, 64, 128], P('req', 'head'), may hold values from -3 to 3
- conv_x_state: float32 [256, 3, 4096], P('req', None, 'head'), may hold values from -6 to 6
- conv_bc_state: float32 [256, 3, 256], P('req'), may hold values from -6 to 6
- slot: int32 [256], replicated, may hold values from 0 to 255, as said below
- lengths: int32 [256], replicated, may hold values from 0 to 16
- accepted: int32 [256], replicated, may hold values from 0 to 16
Outputs:
- out: bfloat16 [256, 16, 2048], P('req', None, 'head')
- new_state: float32 [256, 64, 64, 128], P('req', 'head')
- new_conv_x: float32 [256, 3, 4096], P('req', None, 'head')
- new_conv_bc: float32 [256, 3, 256], P('req')
The draws below stay inside these ranges and needn't reach their ends.
Inputs may be any that keep to these rules, and one draw needn't show every extreme that they name: slot is a permutation of the pool rows; the requests of each aligned block of 32 requests have exactly 4 pool rows in each aligned block of 32 pool rows.
All inputs are finite; a program needn't handle non-finite values.
Results may differ from the reference program's by a relative error of at most 0.0082.
Values may be sent and summed in bfloat16 or wider, within the bound.
A program may use at most 128 MiB of HBM per device.

```python
import math
import jax
import jax.numpy as jnp
from jax import lax

D = 2048
H = 64
P_SIZE = 64
N = 128
K = 4
L = 16
REQ_DEV = 32
DI = 4096
REQUESTS = 256


def draw_slot(key, part):
    blocks = REQUESTS // REQ_DEV
    per_peer = REQ_DEV // blocks
    owner_key, request_key = jax.random.split(jax.random.fold_in(key, 7))
    owner_perm = jax.vmap(lambda sub: jax.random.permutation(sub, REQ_DEV))(jax.random.split(owner_key, blocks))
    request_perm = jax.vmap(lambda sub: jax.random.permutation(sub, REQ_DEV))(jax.random.split(request_key, blocks))
    places = jnp.arange(REQ_DEV, dtype=jnp.int32)
    owners = places // per_peer
    within = places % per_peer
    block_ids = jnp.arange(blocks, dtype=jnp.int32)
    columns = block_ids[:, None] * per_peer + within[None, :]
    values = owners[None, :] * REQ_DEV + owner_perm[owners[None, :], columns].astype(jnp.int32)
    targets = block_ids[:, None] * REQ_DEV + request_perm.astype(jnp.int32)
    return jnp.zeros((REQUESTS,), jnp.int32).at[targets.reshape(-1)].set(values.reshape(-1))


def with_ends(array, stream_key, smallest, top_value):
    place = [jax.random.randint(jax.random.fold_in(stream_key, axis), (), 0, length) for axis, length in enumerate(array.shape)]
    widest = array.shape.index(max(array.shape))
    neighbour = place[:widest] + [(place[widest] + 1) % array.shape[widest]] + place[widest + 1:]
    return array.at[tuple(place)].set(smallest).at[tuple(neighbour)].set(top_value)


def levels(key, shape, pieces, smallest, top_value):
    factor_of, own = 1.0, jax.random.fold_in(key, 6)
    for axis_at, parts in pieces:
        steps = jnp.exp(jax.random.uniform(jax.random.fold_in(own, axis_at), (parts,), jnp.float32, smallest / len(pieces), top_value / len(pieces)))
        factor_of = factor_of * jnp.repeat(steps, shape[axis_at] // parts).reshape([-1 if axis == axis_at else 1 for axis in range(len(shape))])
    return factor_of


def bell_draw(own_key, shape, scale, most, cuts=(), kind=jnp.bfloat16):
    array = jax.random.normal(own_key, shape, jnp.float32) * scale
    if len(cuts) > 0:
        array = levels(own_key, shape, cuts, -0.22, 0.18) * array
    return jnp.clip(array, min=-most, max=most).astype(kind)


def setup_inputs(seed: int = 0) -> dict:
    key_of = jax.random.split(jax.random.key(seed), 18)
    hidden = bell_draw(key_of[0], (REQUESTS, L, D), 1.0, 6.0, ((0, 8), (2, 4)))
    w_zx = bell_draw(key_of[1], (D, 2, DI), D ** -0.5, 0.125, ((2, 4),))
    w_bc = bell_draw(key_of[2], (D, 2 * N), D ** -0.5, 0.125)
    w_dt = bell_draw(key_of[3], (D, H), D ** -0.5, 0.125, ((1, 4),))
    conv_x_w = bell_draw(key_of[4], (K + 1, DI), 0.5, 3.0, ((1, 4),), jnp.float32)
    conv_bc_w = bell_draw(key_of[5], (K + 1, 2 * N), 0.5, 3.0, (), jnp.float32)
    dt_bias = jnp.clip(-4.0 + 4.5 * jax.random.uniform(key_of[6], (H,), jnp.float32) ** levels(key_of[6], (H,), ((0, 4),), -0.2, 0.2), -4.0, 0.5)
    a_log = jnp.clip(2.5 * jax.random.uniform(key_of[7], (H,), jnp.float32) ** levels(key_of[7], (H,), ((0, 4),), -0.2, 0.2), 0.0, 2.5)
    d_skip = jnp.clip(0.5 + 1.0 * jax.random.uniform(key_of[8], (H,), jnp.float32) ** levels(key_of[8], (H,), ((0, 4),), -0.2, 0.2), 0.5, 1.5)
    norm_gain = jnp.clip(1.0 + 0.18 * jax.random.normal(key_of[9], (DI,), jnp.float32), 0.1, 1.9)
    w_out = bell_draw(key_of[10], (DI, D), DI ** -0.5, 0.09375, ((0, 4),))
    ssm_state = bell_draw(key_of[11], (REQUESTS, H, P_SIZE, N), 0.3, 3.0, ((0, 8), (1, 4)), jnp.float32)
    conv_x_state = bell_draw(key_of[12], (REQUESTS, K - 1, DI), 1.0, 6.0, ((0, 8), (2, 4)), jnp.float32)
    conv_bc_state = bell_draw(key_of[13], (REQUESTS, K - 1, 2 * N), 1.0, 6.0, ((0, 8),), jnp.float32)
    slot = draw_slot(jax.random.fold_in(key_of[17], 71), 0)
    lengths = with_ends(jax.random.randint(key_of[15], (REQUESTS,), 0, L + 1), jax.random.fold_in(key_of[15], 1), 0, L).astype(jnp.int32)
    accepted = with_ends(jax.random.randint(key_of[16], (REQUESTS,), 0, L + 1), jax.random.fold_in(key_of[16], 1), 0, L).astype(jnp.int32)
    return dict(hidden=hidden, w_zx=w_zx, w_bc=w_bc, w_dt=w_dt, conv_x_w=conv_x_w, conv_bc_w=conv_bc_w, dt_bias=dt_bias, a_log=a_log, d_skip=d_skip, norm_gain=norm_gain, w_out=w_out, ssm_state=ssm_state, conv_x_state=conv_x_state, conv_bc_state=conv_bc_state, slot=slot, lengths=lengths, accepted=accepted)


highest = lax.Precision.HIGHEST

def conv_step(previous, inputs, taps):
    window = jnp.concatenate([previous, inputs.astype(jnp.float32)], axis=1)
    tail = taps.shape[0] - 1
    steps = inputs.shape[1]
    total = taps[tail] + taps[0] * window[:, 0:steps]
    for tap in range(1, tail):
        total = total + taps[tap] * window[:, tap:tap + steps]
    return (jax.nn.silu(total).astype(jnp.bfloat16), window)

def keep_rows(window, counted, tail):
    picks = counted[:, None] + jnp.arange(tail, dtype=jnp.int32)[None, :]
    return jnp.take_along_axis(window, picks[:, :, None], axis=1)

def scan_block(x_conv, bc_conv, dt_in, states, counted, dt_bias, a_log, d_skip):
    heads = states.shape[1]
    nstate = states.shape[3]
    blocks, steps, chans = x_conv.shape
    headdim = chans // heads
    xh = x_conv.astype(jnp.float32).reshape(blocks, steps, heads, headdim)
    bmat = bc_conv[..., :nstate].astype(jnp.float32)
    cmat = bc_conv[..., nstate:].astype(jnp.float32)
    step_size = jax.nn.softplus(dt_in.astype(jnp.float32) + dt_bias)
    rate = step_size * -jnp.exp(a_log)
    cumul = jnp.cumsum(rate, axis=1)
    carried = jnp.exp(cumul)[..., None] * jnp.einsum('bhpn,btn->bthp', states, cmat, precision=highest)
    inner = jnp.einsum('btn,bsn->bts', cmat, bmat, precision=highest)
    places = jnp.arange(steps, dtype=jnp.int32)
    lower = (places[:, None] >= places[None, :])[None, :, :, None]
    spread = cumul[:, :, None, :] - cumul[:, None, :, :]
    factor = jnp.where(lower, jnp.exp(jnp.where(lower, spread, 0.0)), 0.0)
    factor = factor * inner[..., None] * step_size[:, None, :, :]
    within = jnp.einsum('btsh,bshp->bthp', factor, xh, precision=highest)
    mixed = (carried + within + d_skip[:, None] * xh).reshape(blocks, steps, chans).astype(jnp.bfloat16)
    live = (places[None, :] < counted[:, None])[..., None]
    total = lax.optimization_barrier(jnp.sum(jnp.where(live, rate, 0.0), axis=1))
    remain = jnp.where(live, total[:, None, :] - cumul, 0.0)
    scaled = jnp.where(live, jnp.exp(remain) * step_size, 0.0)
    updated = jnp.exp(total)[:, :, None, None] * states
    updated = updated + jnp.einsum('bsh,bshp,bsn->bhpn', scaled, xh, bmat, precision=highest)
    return (mixed, updated)

def reference(hidden, w_zx, w_bc, w_dt, conv_x_w, conv_bc_w, dt_bias, a_log, d_skip, norm_gain, w_out, ssm_state, conv_x_state, conv_bc_state, slot, lengths, accepted):
    requests, steps, width = hidden.shape
    inner = w_zx.shape[2]
    bc_cols = w_bc.shape[1]
    tail = conv_x_state.shape[1]
    counted = jnp.minimum(accepted, lengths).astype(jnp.int32)
    holder = jnp.argsort(slot).astype(jnp.int32)
    stacked = jnp.concatenate([w_zx.reshape(width, 2 * inner), w_bc, w_dt], axis=1)
    group_size = math.gcd(requests, 16)

    def one_group(pool_rows):
        request_ids = holder[pool_rows]
        tokens = hidden[request_ids]
        projected = jnp.dot(tokens.reshape(-1, width), stacked, preferred_element_type=jnp.float32)
        projected = projected.astype(jnp.bfloat16).reshape(group_size, steps, -1)
        gate_in = projected[..., :inner]
        x_in = projected[..., inner:2 * inner]
        bc_in = projected[..., 2 * inner:2 * inner + bc_cols]
        dt_in = projected[..., 2 * inner + bc_cols:]
        mine = counted[request_ids]
        x_conv, x_window = conv_step(conv_x_state[pool_rows], x_in, conv_x_w)
        bc_conv, bc_window = conv_step(conv_bc_state[pool_rows], bc_in, conv_bc_w)
        mixed, updated = scan_block(x_conv, bc_conv, dt_in, ssm_state[pool_rows], mine, dt_bias, a_log, d_skip)
        gated = mixed.astype(jnp.float32) * jax.nn.silu(gate_in.astype(jnp.float32))
        meansq = lax.optimization_barrier(jnp.mean(gated * gated, axis=-1, keepdims=True))
        normed = (gated * lax.rsqrt(meansq + 1e-05) * norm_gain).astype(jnp.bfloat16)
        result = jnp.dot(normed.reshape(-1, inner), w_out, preferred_element_type=jnp.float32).reshape(group_size, steps, width)
        places = jnp.arange(steps, dtype=jnp.int32)
        valid = places[None, :] < lengths[request_ids][:, None]
        result = jnp.where(valid[..., None], result, 0.0).astype(jnp.bfloat16)
        return (result, updated, keep_rows(x_window, mine, tail), keep_rows(bc_window, mine, tail))
    pool_groups = jnp.arange(requests, dtype=jnp.int32).reshape(-1, group_size)
    out_pool, states_new, conv_x_new, conv_bc_new = lax.map(one_group, pool_groups)
    out_pool = out_pool.reshape(requests, steps, width)
    out = out_pool[slot]
    return (out, states_new.reshape(ssm_state.shape), conv_x_new.reshape(conv_x_state.shape), conv_bc_new.reshape(conv_bc_state.shape))
```

```python
import functools

import jax
import jax.numpy as jnp
from jax import lax
from jax.experimental import pallas as pl
from jax.experimental.pallas import tpu as pltpu
from jax.sharding import PartitionSpec as P

highest = lax.Precision.HIGHEST
f32 = jnp.float32
bf16 = jnp.bfloat16


def iota(shape, dim):
    return lax.broadcasted_iota(jnp.int32, shape, dim)


def dot_nt(a, b):
    return lax.dot_general(a, b, (((1,), (1,)), ((), ())), preferred_element_type=f32)


def dot_nn(a, b, precision=None):
    return jnp.dot(a, b, preferred_element_type=f32, precision=precision)


def silu(v):
    return v * (1.0 / (1.0 + jnp.exp(-v)))


def conv(window_ref, prev_ref, inputs, taps, keep_ref, count_of, group, steps, tail):
    base = 8 - tail
    chans = inputs.shape[-1]
    window_ref[:, 0:8, :] = jnp.zeros((group, 8, inputs.shape[-1]), f32)
    window_ref[:, base:8, :] = prev_ref[...]
    window_ref[:, 8 : 8 + steps, :] = inputs.reshape(group, steps, chans)
    total = taps[tail + 1 : tail + 2, :][None]
    for tap in range(tail + 1):
        total = total + taps[tap : tap + 1, :][None] * window_ref[:, base + tap : base + tap + steps, :]
    for r in range(group):
        held = window_ref[r, :, :]
        place = iota((8 + steps, 1), 0) - base - count_of(r)
        for k in range(tail):
            keep_ref[r, k : k + 1, :] = jnp.sum(jnp.where(place == k, held, 0.0), axis=0, keepdims=True)
    return silu(total).astype(bf16).reshape(group * steps, chans)


def core_kernel(
    group,
    counted_ref,
    zx_ref,
    bcdt_ref,
    state_ref,
    cx_ref,
    cbc_ref,
    cxw_ref,
    cbw_ref,
    heads_ref,
    gain_ref,
    g_ref,
    sq_ref,
    new_state_ref,
    ncx_ref,
    ncbc_ref,
    xwin,
    bcwin,
):
    heads, headdim, nstate = state_ref.shape[1:]
    chans = heads * headdim
    tokens = zx_ref.shape[0]
    steps = tokens // group
    tail = cx_ref.shape[1]
    first = pl.program_id(0) * group

    def count_of(r):
        return counted_ref[first + r]

    bcdt = bcdt_ref[...].astype(f32)
    x = conv(xwin, cx_ref, zx_ref[:, chans:].astype(f32), cxw_ref[...], ncx_ref, count_of, group, steps, tail)
    bc = conv(bcwin, cbc_ref, bcdt[:, : 2 * nstate], cbw_ref[...], ncbc_ref, count_of, group, steps, tail)
    bmat, cmat = bc[:, :nstate], bc[:, nstate:]
    xf = x.astype(f32)

    dt_bias, a_log, d_skip = heads_ref[0:1, :], heads_ref[1:2, :], heads_ref[2:3, :]
    raw = bcdt[:, 2 * nstate :] + dt_bias
    dt = jnp.maximum(raw, 0.0) + jnp.log1p(jnp.exp(-jnp.abs(raw)))
    rate = dt * -jnp.exp(a_log)

    row, col = iota((tokens, tokens), 0), iota((tokens, tokens), 1)
    same = row // steps == col // steps
    lower = jnp.where(same & (row >= col), 1.0, 0.0)
    cumul = dot_nn(lower, rate, highest)
    token = iota((tokens, heads), 0)
    limit = jnp.zeros((tokens, heads), jnp.int32)
    for r in range(group):
        limit = jnp.where(token // steps == r, count_of(r), limit)
    live = (token % steps) < limit
    total = dot_nn(jnp.where(same, 1.0, 0.0), jnp.where(live, rate, 0.0), highest)
    scaled = jnp.where(live, jnp.exp(jnp.where(live, total - cumul, 0.0)) * dt, 0.0)
    spread_to = jnp.where(iota((heads, chans), 1) // headdim == iota((heads, chans), 0), 1.0, 0.0).astype(bf16)
    dt_e = dot_nn(dt.astype(bf16), spread_to)
    scaled_e = dot_nn(scaled.astype(bf16), spread_to)
    carry_e = dot_nn(jnp.exp(cumul).astype(bf16), spread_to)
    skip_hi = d_skip.astype(bf16)
    skip_lo = (d_skip - skip_hi.astype(f32)).astype(bf16)
    skip_e = dot_nn(jnp.broadcast_to(skip_hi, (8, heads)), spread_to) + dot_nn(
        jnp.broadcast_to(skip_lo, (8, heads)), spread_to
    )
    mixed_skip = skip_e[0:1, :] * xf
    dtx = (dt_e * xf).astype(bf16)
    sxt = (scaled_e * xf).T.astype(bf16)
    btok = iota((tokens, nstate), 0) // steps
    bsel = jnp.concatenate([jnp.where(btok == r, bmat.astype(f32), 0.0) for r in range(group)], axis=1).astype(bf16)
    grown = dot_nn(sxt, bsel)

    wide = heads * steps
    spread_hs = jnp.where(iota((heads, wide), 1) // steps == iota((heads, wide), 0), 1.0, 0.0)
    cumul_hs = dot_nn(cumul, spread_hs, highest)
    t_at, s_at = iota((steps, wide), 0), iota((steps, wide), 1) % steps
    block = (iota((wide, chans), 0) // steps == iota((wide, chans), 1) // headdim).astype(f32).astype(bf16)
    eye = iota((heads, heads), 0) == iota((heads, heads), 1)

    pieces = []
    for r in range(group):
        span = slice(r * steps, (r + 1) * steps)
        c_r = cmat[span, :]
        b_r = bmat[span, :]
        inner = dot_nt(c_r, jnp.concatenate([b_r] * heads, axis=0))
        here = cumul_hs[span, :]
        there = jnp.sum(jnp.where(t_at == s_at, here, 0.0), axis=0, keepdims=True)
        factor = jnp.where(t_at >= s_at, jnp.exp(jnp.where(t_at >= s_at, here - there, 0.0)) * inner, 0.0)
        spreaded = jnp.concatenate([dtx[span, :]] * heads, axis=0) * block
        within = dot_nn(factor.astype(bf16), spreaded)
        states = state_ref[r].reshape(chans, nstate)
        carried = dot_nt(c_r, states.astype(bf16))
        pieces.append(carry_e[span, :] * carried + within)
        decay = jnp.sum(jnp.where(eye, jnp.exp(total[r * steps : r * steps + 1, :]), 0.0), axis=1, keepdims=True)
        for h in range(heads):
            new_state_ref[r, h] = (
                state_ref[r, h] * decay[h : h + 1, :]
                + grown[h * headdim : (h + 1) * headdim, r * nstate : (r + 1) * nstate]
            )
    mixed = (jnp.concatenate(pieces, axis=0) + mixed_skip).astype(bf16).astype(f32)
    gated = mixed * silu(zx_ref[:, :chans].astype(f32))
    sq_ref[...] = jnp.sum(gated * gated, axis=1, keepdims=True)
    g_ref[...] = (gated * gain_ref[...]).astype(bf16)


def core(counted, zx, bcdt, states, cx, cbc, cxw, cbw, head_params, gain, group):
    rows, heads, headdim, nstate = states.shape
    chans = heads * headdim
    steps = zx.shape[0] // rows
    tail = cx.shape[1]
    tokens = group * steps

    def step_block(*shape):
        return pl.BlockSpec(shape, lambda i, c: (i,) + (0,) * (len(shape) - 1))

    def whole(a):
        return pl.BlockSpec(a.shape, lambda i, c: (0,) * a.ndim)

    return pl.pallas_call(
        functools.partial(core_kernel, group),
        grid_spec=pltpu.PrefetchScalarGridSpec(
            num_scalar_prefetch=1,
            grid=(rows // group,),
            in_specs=[
                step_block(tokens, 2 * chans),
                step_block(tokens, bcdt.shape[1]),
                step_block(group, heads, headdim, nstate),
                step_block(group, tail, chans),
                step_block(group, tail, 2 * nstate),
                whole(cxw),
                whole(cbw),
                whole(head_params),
                whole(gain),
            ],
            out_specs=[
                step_block(tokens, chans),
                step_block(tokens, 1),
                step_block(group, heads, headdim, nstate),
                step_block(group, tail, chans),
                step_block(group, tail, 2 * nstate),
            ],
            scratch_shapes=[
                pltpu.VMEM((group, 8 + steps, chans), f32),
                pltpu.VMEM((group, 8 + steps, 2 * nstate), f32),
            ],
        ),
        out_shape=[
            jax.ShapeDtypeStruct((rows * steps, chans), bf16),
            jax.ShapeDtypeStruct((rows * steps, 1), f32),
            jax.ShapeDtypeStruct(states.shape, f32),
            jax.ShapeDtypeStruct(cx.shape, f32),
            jax.ShapeDtypeStruct(cbc.shape, f32),
        ],
        compiler_params=pltpu.CompilerParams(vmem_limit_bytes=48 * 1024 * 1024),
        name="core",
    )(counted, zx, bcdt, states, cx, cbc, cxw, cbw, head_params, gain)


def routes(slot, rows, myself, peers):
    per_peer = rows // peers
    blocks = slot.reshape(peers, rows)
    owner = blocks // rows
    earlier = jnp.arange(rows)[None, :, None] > jnp.arange(rows)[None, None, :]
    rank = jnp.sum((owner[:, :, None] == owner[:, None, :]) & earlier, axis=2, dtype=jnp.int32)
    places = jnp.arange(rows, dtype=jnp.int32)
    my_owner = lax.dynamic_index_in_dim(owner, myself, 0, keepdims=False)
    my_rank = lax.dynamic_index_in_dim(rank, myself, 0, keepdims=False)
    home = my_owner * per_peer + my_rank
    send_order = jnp.sum(jnp.where(home[None, :] == places[:, None], places[None, :], 0), axis=1, dtype=jnp.int32)
    arrive = (jnp.arange(peers, dtype=jnp.int32)[:, None] * per_peer + rank).reshape(-1)
    flat = slot.reshape(-1)
    hit = flat[None, :] == (myself * rows + places)[:, None]
    to_pool = jnp.sum(jnp.where(hit, arrive[None, :], 0), axis=1, dtype=jnp.int32)
    request = jnp.sum(jnp.where(hit, jnp.arange(flat.shape[0], dtype=jnp.int32)[None, :], 0), axis=1, dtype=jnp.int32)
    back_order = jnp.sum(jnp.where(to_pool[None, :] == places[:, None], places[None, :], 0), axis=1, dtype=jnp.int32)
    return send_order, to_pool, back_order, home, request


def per_device(
    hidden,
    w_zx,
    w_bc,
    w_dt,
    conv_x_w,
    conv_bc_w,
    dt_bias,
    a_log,
    d_skip,
    norm_gain,
    w_out,
    ssm_state,
    conv_x_state,
    conv_bc_state,
    slot,
    lengths,
    accepted,
):
    rows, steps, width_part = hidden.shape
    width = w_zx.shape[0]
    chans = w_zx.shape[2]
    myself = lax.axis_index("req")
    peers = lax.axis_size("req")
    send_order, to_pool, back_order, home, request = routes(slot, rows, myself, peers)
    counted = jnp.minimum(accepted, lengths)
    hit = jnp.arange(slot.shape[0], dtype=jnp.int32)[None, :] == request[:, None]
    my_counted = jnp.sum(jnp.where(hit, counted[None, :], 0), axis=1, dtype=jnp.int32)

    outgoing = jnp.take(hidden, send_order, axis=0)
    arrived = lax.all_to_all(outgoing, "req", split_axis=0, concat_axis=0, tiled=True)
    pooled = jnp.take(arrived, to_pool, axis=0)
    tokens = lax.all_gather(pooled, "head", axis=2, tiled=True).reshape(rows * steps, width)
    zx = jnp.dot(tokens, w_zx.reshape(width, 2 * chans), preferred_element_type=f32).astype(bf16)
    bcdt = jnp.dot(tokens, jnp.concatenate([w_bc, w_dt], axis=1), preferred_element_type=f32).astype(bf16)
    g, squares, new_state, new_conv_x, new_conv_bc = core(
        my_counted,
        zx,
        bcdt,
        ssm_state,
        conv_x_state,
        conv_bc_state,
        conv_x_w,
        conv_bc_w,
        jnp.stack([dt_bias, a_log, d_skip]),
        norm_gain[None, :],
        4,
    )
    partial_out = jnp.dot(g, w_out, preferred_element_type=f32).astype(bf16)
    summed = lax.psum_scatter(partial_out, "head", scatter_dimension=1, tiled=True)
    meansq = lax.psum(squares, "head") / (chans * lax.axis_size("head"))
    result = (summed.astype(f32) * lax.rsqrt(meansq + 1e-05)).astype(bf16).reshape(rows, steps, width_part)
    back = lax.all_to_all(jnp.take(result, back_order, axis=0), "req", split_axis=0, concat_axis=0, tiled=True)
    mine = jnp.take(back, home, axis=0)
    my_lengths = lax.dynamic_slice_in_dim(lengths, myself * rows, rows, 0)
    valid = jnp.arange(steps, dtype=jnp.int32)[None, :] < my_lengths[:, None]
    out = jnp.where(valid[..., None], mine, jnp.zeros((), bf16))
    return (out, new_state, new_conv_x, new_conv_bc)


def solution(mesh):
    in_specs = (
        P("req", None, "head"),
        P(None, None, "head"),
        P(),
        P(None, "head"),
        P(None, "head"),
        P(),
        P("head"),
        P("head"),
        P("head"),
        P("head"),
        P("head", None),
        P("req", "head", None, None),
        P("req", None, "head"),
        P("req", None, None),
        P(),
        P(),
        P(),
    )
    out_specs = (
        P("req", None, "head"),
        P("req", "head", None, None),
        P("req", None, "head"),
        P("req", None, None),
    )
    return jax.shard_map(
        per_device, mesh=mesh, in_specs=in_specs, out_specs=out_specs, check_vma=False
    )
```

```python
import functools

import jax
import jax.numpy as jnp
from jax import lax
from jax.experimental import pallas as pl
from jax.experimental.pallas import tpu as pltpu
from jax.sharding import PartitionSpec as P

highest = lax.Precision.HIGHEST
f32 = jnp.float32
bf16 = jnp.bfloat16


def iota(shape, dim):
    return lax.broadcasted_iota(jnp.int32, shape, dim)


def dot_nt(a, b):
    return lax.dot_general(a, b, (((1,), (1,)), ((), ())), preferred_element_type=f32)


def dot_nn(a, b, precision=None):
    return jnp.dot(a, b, preferred_element_type=f32, precision=precision)


def silu(v):
    return v * (1.0 / (1.0 + jnp.exp(-v)))


def conv(window_ref, prev_ref, inputs, taps, keep_ref, count_of, group, steps, tail):
    base = 8 - tail
    chans = inputs.shape[-1]
    window_ref[:, 0:8, :] = jnp.zeros((group, 8, inputs.shape[-1]), f32)
    window_ref[:, base:8, :] = prev_ref[...]
    window_ref[:, 8 : 8 + steps, :] = inputs.reshape(group, steps, chans)
    total = taps[tail + 1 : tail + 2, :][None]
    for tap in range(tail + 1):
        total = total + taps[tap : tap + 1, :][None] * window_ref[:, base + tap : base + tap + steps, :]
    for r in range(group):
        held = window_ref[r, :, :]
        place = iota((8 + steps, 1), 0) - base - count_of(r)
        for k in range(tail):
            keep_ref[r, k : k + 1, :] = jnp.sum(jnp.where(place == k, held, 0.0), axis=0, keepdims=True)
    return silu(total).astype(bf16).reshape(group * steps, chans)


def core_kernel(
    group,
    offset,
    counted_ref,
    zx_ref,
    bcdt_ref,
    state_ref,
    cx_ref,
    cbc_ref,
    cxw_ref,
    cbw_ref,
    heads_ref,
    gain_ref,
    *refs,
):
    (g_ref, sq_ref, new_state_ref, ncx_ref, ncbc_ref, xwin, bcwin) = refs[-7:]
    heads, headdim, nstate = state_ref.shape[1:]
    chans = heads * headdim
    tokens = zx_ref.shape[0]
    steps = tokens // group
    tail = cx_ref.shape[1]
    first = (pl.program_id(0) + offset) * group

    def count_of(r):
        return counted_ref[first + r]

    bcdt = bcdt_ref[...].astype(f32)
    x = conv(xwin, cx_ref, zx_ref[:, chans:].astype(f32), cxw_ref[...], ncx_ref, count_of, group, steps, tail)
    bc = conv(bcwin, cbc_ref, bcdt[:, : 2 * nstate], cbw_ref[...], ncbc_ref, count_of, group, steps, tail)
    bmat, cmat = bc[:, :nstate], bc[:, nstate:]
    xf = x.astype(f32)

    dt_bias, a_log, d_skip = heads_ref[0:1, :], heads_ref[1:2, :], heads_ref[2:3, :]
    raw = bcdt[:, 2 * nstate :] + dt_bias
    dt = jnp.maximum(raw, 0.0) + jnp.log1p(jnp.exp(-jnp.abs(raw)))
    rate = dt * -jnp.exp(a_log)

    row, col = iota((tokens, tokens), 0), iota((tokens, tokens), 1)
    same = row // steps == col // steps
    lower = jnp.where(same & (row >= col), 1.0, 0.0)
    cumul = dot_nn(lower, rate, highest)
    token = iota((tokens, heads), 0)
    limit = jnp.zeros((tokens, heads), jnp.int32)
    for r in range(group):
        limit = jnp.where(token // steps == r, count_of(r), limit)
    live = (token % steps) < limit
    total = dot_nn(jnp.where(same, 1.0, 0.0), jnp.where(live, rate, 0.0), highest)
    scaled = jnp.where(live, jnp.exp(jnp.where(live, total - cumul, 0.0)) * dt, 0.0)
    spread_to = jnp.where(iota((heads, chans), 1) // headdim == iota((heads, chans), 0), 1.0, 0.0).astype(bf16)
    dt_e = dot_nn(dt.astype(bf16), spread_to)
    scaled_e = dot_nn(scaled.astype(bf16), spread_to)
    carry_e = dot_nn(jnp.exp(cumul).astype(bf16), spread_to)
    skip_hi = d_skip.astype(bf16)
    skip_lo = (d_skip - skip_hi.astype(f32)).astype(bf16)
    skip_e = dot_nn(jnp.broadcast_to(skip_hi, (8, heads)), spread_to) + dot_nn(
        jnp.broadcast_to(skip_lo, (8, heads)), spread_to
    )
    mixed_skip = skip_e[0:1, :] * xf
    dtx = (dt_e * xf).astype(bf16)
    sxt = (scaled_e * xf).T.astype(bf16)
    btok = iota((tokens, nstate), 0) // steps
    bsel = jnp.concatenate([jnp.where(btok == r, bmat.astype(f32), 0.0) for r in range(group)], axis=1).astype(bf16)
    grown = dot_nn(sxt, bsel)

    wide = heads * steps
    spread_hs = jnp.where(iota((heads, wide), 1) // steps == iota((heads, wide), 0), 1.0, 0.0)
    cumul_hs = dot_nn(cumul, spread_hs, highest)
    t_at, s_at = iota((steps, wide), 0), iota((steps, wide), 1) % steps
    block = (iota((wide, chans), 0) // steps == iota((wide, chans), 1) // headdim).astype(f32).astype(bf16)
    eye = iota((heads, heads), 0) == iota((heads, heads), 1)

    pieces = []
    for r in range(group):
        span = slice(r * steps, (r + 1) * steps)
        c_r = cmat[span, :]
        b_r = bmat[span, :]
        inner = dot_nt(c_r, jnp.concatenate([b_r] * heads, axis=0))
        here = cumul_hs[span, :]
        there = jnp.sum(jnp.where(t_at == s_at, here, 0.0), axis=0, keepdims=True)
        factor = jnp.where(t_at >= s_at, jnp.exp(jnp.where(t_at >= s_at, here - there, 0.0)) * inner, 0.0)
        spreaded = jnp.concatenate([dtx[span, :]] * heads, axis=0) * block
        within = dot_nn(factor.astype(bf16), spreaded)
        states = state_ref[r].reshape(chans, nstate)
        carried = dot_nt(c_r, states.astype(bf16))
        pieces.append(carry_e[span, :] * carried + within)
        decay = jnp.sum(jnp.where(eye, jnp.exp(total[r * steps : r * steps + 1, :]), 0.0), axis=1, keepdims=True)
        for h in range(heads):
            new_state_ref[r, h] = (
                state_ref[r, h] * decay[h : h + 1, :]
                + grown[h * headdim : (h + 1) * headdim, r * nstate : (r + 1) * nstate]
            )
    mixed = (jnp.concatenate(pieces, axis=0) + mixed_skip).astype(bf16).astype(f32)
    gated = mixed * silu(zx_ref[:, :chans].astype(f32))
    sq_ref[...] = jnp.sum(gated * gated, axis=1, keepdims=True)
    g_ref[...] = (gated * gain_ref[...]).astype(bf16)


def core(counted, zx, bcdt, states, cx, cbc, cxw, cbw, head_params, gain, group, chunk, chunks, done):
    rows, heads, headdim, nstate = states.shape
    chans = heads * headdim
    steps = zx.shape[0] * chunks // rows
    tail = cx.shape[1]
    tokens = group * steps
    calls = rows // group // chunks
    offset = chunk * calls

    def step_block(*shape):
        return pl.BlockSpec(shape, lambda i, c: (i,) + (0,) * (len(shape) - 1))

    def pool_block(*shape):
        return pl.BlockSpec(shape, lambda i, c: (i + offset,) + (0,) * (len(shape) - 1))

    def whole(a):
        return pl.BlockSpec(a.shape, lambda i, c: (0,) * a.ndim)

    return pl.pallas_call(
        functools.partial(core_kernel, group, offset),
        grid_spec=pltpu.PrefetchScalarGridSpec(
            num_scalar_prefetch=1,
            grid=(calls,),
            in_specs=[
                step_block(tokens, 2 * chans),
                step_block(tokens, bcdt.shape[1]),
                pool_block(group, heads, headdim, nstate),
                pool_block(group, tail, chans),
                pool_block(group, tail, 2 * nstate),
                whole(cxw),
                whole(cbw),
                whole(head_params),
                whole(gain),
            ]
            + [pl.BlockSpec(memory_space=pl.ANY)] * len(done),
            out_specs=[
                step_block(tokens, chans),
                step_block(tokens, 1),
                pool_block(group, heads, headdim, nstate),
                pool_block(group, tail, chans),
                pool_block(group, tail, 2 * nstate),
            ],
            scratch_shapes=[
                pltpu.VMEM((group, 8 + steps, chans), f32),
                pltpu.VMEM((group, 8 + steps, 2 * nstate), f32),
            ],
        ),
        out_shape=[
            jax.ShapeDtypeStruct((zx.shape[0], chans), bf16),
            jax.ShapeDtypeStruct((zx.shape[0], 1), f32),
            jax.ShapeDtypeStruct(states.shape, f32),
            jax.ShapeDtypeStruct(cx.shape, f32),
            jax.ShapeDtypeStruct(cbc.shape, f32),
        ],
        input_output_aliases={10 + k: 2 + k for k in range(len(done))},
        compiler_params=pltpu.CompilerParams(vmem_limit_bytes=40 * 1024 * 1024),
        cost_estimate=pl.CostEstimate(
            flops=2 * zx.shape[0] * chans * nstate * 8,
            bytes_accessed=8 * (rows // chunks) * chans * nstate,
            transcendentals=zx.shape[0] * chans * 2,
        ),
        name="core",
    )(counted, zx, bcdt, states, cx, cbc, cxw, cbw, head_params, gain, *done)


def routes(slot, rows, myself, peers):
    per_peer = rows // peers
    blocks = slot.reshape(peers, rows)
    owner = blocks // rows
    earlier = jnp.arange(rows)[None, :, None] > jnp.arange(rows)[None, None, :]
    rank = jnp.sum((owner[:, :, None] == owner[:, None, :]) & earlier, axis=2, dtype=jnp.int32)
    places = jnp.arange(rows, dtype=jnp.int32)
    my_owner = lax.dynamic_index_in_dim(owner, myself, 0, keepdims=False)
    my_rank = lax.dynamic_index_in_dim(rank, myself, 0, keepdims=False)
    home = my_owner * per_peer + my_rank
    send_order = jnp.sum(jnp.where(home[None, :] == places[:, None], places[None, :], 0), axis=1, dtype=jnp.int32)
    arrive = (jnp.arange(peers, dtype=jnp.int32)[:, None] * per_peer + rank).reshape(-1)
    flat = slot.reshape(-1)
    hit = flat[None, :] == (myself * rows + places)[:, None]
    to_pool = jnp.sum(jnp.where(hit, arrive[None, :], 0), axis=1, dtype=jnp.int32)
    request = jnp.sum(jnp.where(hit, jnp.arange(flat.shape[0], dtype=jnp.int32)[None, :], 0), axis=1, dtype=jnp.int32)
    back_order = jnp.sum(jnp.where(to_pool[None, :] == places[:, None], places[None, :], 0), axis=1, dtype=jnp.int32)
    return send_order, to_pool, back_order, home, request


def per_device(
    hidden,
    w_zx,
    w_bc,
    w_dt,
    conv_x_w,
    conv_bc_w,
    dt_bias,
    a_log,
    d_skip,
    norm_gain,
    w_out,
    ssm_state,
    conv_x_state,
    conv_bc_state,
    slot,
    lengths,
    accepted,
):
    rows, steps, width_part = hidden.shape
    width = w_zx.shape[0]
    chans = w_zx.shape[2]
    myself = lax.axis_index("req")
    peers = lax.axis_size("req")
    send_order, to_pool, back_order, home, request = routes(slot, rows, myself, peers)
    counted = jnp.minimum(accepted, lengths)
    hit = jnp.arange(slot.shape[0], dtype=jnp.int32)[None, :] == request[:, None]
    my_counted = jnp.sum(jnp.where(hit, counted[None, :], 0), axis=1, dtype=jnp.int32)

    outgoing = jnp.take(hidden, send_order, axis=0)
    arrived = lax.all_to_all(outgoing, "req", split_axis=0, concat_axis=0, tiled=True)
    pooled = jnp.take(arrived, to_pool, axis=0)
    chunks = 2
    part = rows // chunks
    flat_zx = w_zx.reshape(width, 2 * chans)
    w_bcdt = jnp.concatenate([w_bc, w_dt], axis=1)
    head_params = jnp.stack([dt_bias, a_log, d_skip])
    hold = lax.optimization_barrier

    gathered = []
    for c in range(chunks):
        piece = pooled[c * part : (c + 1) * part]
        if c > 0:
            gathered[-1], piece = hold((gathered[-1], piece))
        gathered.append(lax.all_gather(piece, "head", axis=2, tiled=True))
    done, squares, summed = (), [], []
    for c in range(chunks):
        tokens = gathered[c].reshape(part * steps, width)
        zx = jnp.dot(tokens, flat_zx, preferred_element_type=f32).astype(bf16)
        bcdt = jnp.dot(tokens, w_bcdt, preferred_element_type=f32).astype(bf16)
        g, sq, *done = core(
            my_counted,
            zx,
            bcdt,
            ssm_state,
            conv_x_state,
            conv_bc_state,
            conv_x_w,
            conv_bc_w,
            head_params,
            norm_gain[None, :],
            4,
            c,
            chunks,
            done,
        )
        squares.append(sq)
        shares = jnp.dot(g, w_out, preferred_element_type=f32).astype(bf16)
        if c > 0:
            summed[-1], shares = hold((summed[-1], shares))
        summed.append(lax.psum_scatter(shares, "head", scatter_dimension=1, tiled=True))
    new_state, new_conv_x, new_conv_bc = done
    square = jnp.concatenate(squares, axis=0).reshape(-1, 128)
    total = jnp.sum(lax.all_gather(square, "head", axis=0), axis=0).reshape(rows * steps, 1)
    meansq = total / (chans * lax.axis_size("head"))
    full = jnp.concatenate(summed, axis=0).astype(f32)
    result = (full * lax.rsqrt(meansq + 1e-05)).astype(bf16).reshape(rows, steps, width_part)
    back = lax.all_to_all(jnp.take(result, back_order, axis=0), "req", split_axis=0, concat_axis=0, tiled=True)
    mine = jnp.take(back, home, axis=0)
    my_lengths = lax.dynamic_slice_in_dim(lengths, myself * rows, rows, 0)
    valid = jnp.arange(steps, dtype=jnp.int32)[None, :] < my_lengths[:, None]
    out = jnp.where(valid[..., None], mine, jnp.zeros((), bf16))
    return (out, new_state, new_conv_x, new_conv_bc)


def solution(mesh):
    in_specs = (
        P("req", None, "head"),
        P(None, None, "head"),
        P(),
        P(None, "head"),
        P(None, "head"),
        P(),
        P("head"),
        P("head"),
        P("head"),
        P("head"),
        P("head", None),
        P("req", "head", None, None),
        P("req", None, "head"),
        P("req", None, None),
        P(),
        P(),
        P(),
    )
    out_specs = (
        P("req", None, "head"),
        P("req", "head", None, None),
        P("req", None, "head"),
        P("req", None, None),
    )
    return jax.shard_map(
        per_device, mesh=mesh, in_specs=in_specs, out_specs=out_specs, check_vma=False
    )
```

```python
import functools

import jax
import jax.numpy as jnp
from jax import lax
from jax.experimental import pallas as pl
from jax.experimental.pallas import tpu as pltpu
from jax.sharding import PartitionSpec as P

highest = lax.Precision.HIGHEST
f32 = jnp.float32
bf16 = jnp.bfloat16


def iota(shape, dim):
    return lax.broadcasted_iota(jnp.int32, shape, dim)


def dot_nt(a, b):
    return lax.dot_general(a, b, (((1,), (1,)), ((), ())), preferred_element_type=f32)


def dot_nn(a, b, precision=None):
    return jnp.dot(a, b, preferred_element_type=f32, precision=precision)


def silu(v):
    return v * (1.0 / (1.0 + jnp.exp(-v)))


def conv(window_ref, prev_ref, inputs, taps, keep_ref, count_of, group, steps, tail):
    base = 8 - tail
    chans = inputs.shape[-1]
    window_ref[:, 0:8, :] = jnp.zeros((group, 8, inputs.shape[-1]), f32)
    window_ref[:, base:8, :] = prev_ref[...]
    window_ref[:, 8 : 8 + steps, :] = inputs.reshape(group, steps, chans)
    total = taps[tail + 1 : tail + 2, :][None]
    for tap in range(tail + 1):
        total = total + taps[tap : tap + 1, :][None] * window_ref[:, base + tap : base + tap + steps, :]
    for r in range(group):
        held = window_ref[r, :, :]
        place = iota((8 + steps, 1), 0) - base - count_of(r)
        for k in range(tail):
            keep_ref[r, k : k + 1, :] = jnp.sum(jnp.where(place == k, held, 0.0), axis=0, keepdims=True)
    return silu(total).astype(bf16).reshape(group * steps, chans)


def core_kernel(
    group,
    offset,
    counted_ref,
    zx_ref,
    bcdt_ref,
    state_ref,
    cx_ref,
    cbc_ref,
    cxw_ref,
    cbw_ref,
    heads_ref,
    gain_ref,
    *refs,
):
    (g_ref, sq_ref, new_state_ref, ncx_ref, ncbc_ref, xwin, bcwin) = refs[-7:]
    heads, headdim, nstate = state_ref.shape[1:]
    chans = heads * headdim
    tokens = zx_ref.shape[0]
    steps = tokens // group
    tail = cx_ref.shape[1]
    first = (pl.program_id(0) + offset) * group

    def count_of(r):
        return counted_ref[first + r]

    bcdt = bcdt_ref[...].astype(f32)
    x = conv(xwin, cx_ref, zx_ref[:, chans:].astype(f32), cxw_ref[...], ncx_ref, count_of, group, steps, tail)
    bc = conv(bcwin, cbc_ref, bcdt[:, : 2 * nstate], cbw_ref[...], ncbc_ref, count_of, group, steps, tail)
    bmat, cmat = bc[:, :nstate], bc[:, nstate:]
    xf = x.astype(f32)

    dt_bias, a_log, d_skip = heads_ref[0:1, :], heads_ref[1:2, :], heads_ref[2:3, :]
    raw = bcdt[:, 2 * nstate :] + dt_bias
    dt = jnp.maximum(raw, 0.0) + jnp.log1p(jnp.exp(-jnp.abs(raw)))
    rate = dt * -jnp.exp(a_log)

    row, col = iota((tokens, tokens), 0), iota((tokens, tokens), 1)
    same = row // steps == col // steps
    lower = jnp.where(same & (row >= col), 1.0, 0.0)
    cumul = dot_nn(lower, rate, highest)
    token = iota((tokens, heads), 0)
    limit = jnp.zeros((tokens, heads), jnp.int32)
    for r in range(group):
        limit = jnp.where(token // steps == r, count_of(r), limit)
    live = (token % steps) < limit
    total = dot_nn(jnp.where(same, 1.0, 0.0), jnp.where(live, rate, 0.0), highest)
    scaled = jnp.where(live, jnp.exp(jnp.where(live, total - cumul, 0.0)) * dt, 0.0)
    spread_to = jnp.where(iota((heads, chans), 1) // headdim == iota((heads, chans), 0), 1.0, 0.0).astype(bf16)
    dt_e = dot_nn(dt.astype(bf16), spread_to)
    scaled_e = dot_nn(scaled.astype(bf16), spread_to)
    carry_e = dot_nn(jnp.exp(cumul).astype(bf16), spread_to)
    skip_hi = d_skip.astype(bf16)
    skip_lo = (d_skip - skip_hi.astype(f32)).astype(bf16)
    skip_e = dot_nn(jnp.broadcast_to(skip_hi, (8, heads)), spread_to) + dot_nn(
        jnp.broadcast_to(skip_lo, (8, heads)), spread_to
    )
    mixed_skip = skip_e[0:1, :] * xf
    dtx = (dt_e * xf).astype(bf16)
    sxt = (scaled_e * xf).T.astype(bf16)
    btok = iota((tokens, nstate), 0) // steps
    bsel = jnp.concatenate([jnp.where(btok == r, bmat.astype(f32), 0.0) for r in range(group)], axis=1).astype(bf16)
    grown = dot_nn(sxt, bsel)

    wide = heads * steps
    spread_hs = jnp.where(iota((heads, wide), 1) // steps == iota((heads, wide), 0), 1.0, 0.0)
    cumul_hs = dot_nn(cumul, spread_hs, highest)
    t_at, s_at = iota((steps, wide), 0), iota((steps, wide), 1) % steps
    block = (iota((wide, chans), 0) // steps == iota((wide, chans), 1) // headdim).astype(f32).astype(bf16)
    eye = iota((heads, heads), 0) == iota((heads, heads), 1)

    pieces = []
    for r in range(group):
        span = slice(r * steps, (r + 1) * steps)
        c_r = cmat[span, :]
        b_r = bmat[span, :]
        inner = dot_nt(c_r, jnp.concatenate([b_r] * heads, axis=0))
        here = cumul_hs[span, :]
        there = jnp.sum(jnp.where(t_at == s_at, here, 0.0), axis=0, keepdims=True)
        factor = jnp.where(t_at >= s_at, jnp.exp(jnp.where(t_at >= s_at, here - there, 0.0)) * inner, 0.0)
        spreaded = jnp.concatenate([dtx[span, :]] * heads, axis=0) * block
        within = dot_nn(factor.astype(bf16), spreaded)
        states = state_ref[r].reshape(chans, nstate)
        carried = dot_nt(c_r, states.astype(bf16))
        pieces.append(carry_e[span, :] * carried + within)
        decay = jnp.sum(jnp.where(eye, jnp.exp(total[r * steps : r * steps + 1, :]), 0.0), axis=1, keepdims=True)
        for h in range(heads):
            new_state_ref[r, h] = (
                state_ref[r, h] * decay[h : h + 1, :]
                + grown[h * headdim : (h + 1) * headdim, r * nstate : (r + 1) * nstate]
            )
    mixed = (jnp.concatenate(pieces, axis=0) + mixed_skip).astype(bf16).astype(f32)
    gated = mixed * silu(zx_ref[:, :chans].astype(f32))
    sq_ref[...] = jnp.sum(gated * gated, axis=1, keepdims=True)
    g_ref[...] = (gated * gain_ref[...]).astype(bf16)


def core(counted, zx, bcdt, states, cx, cbc, cxw, cbw, head_params, gain, group, chunk, chunks, done):
    rows, heads, headdim, nstate = states.shape
    chans = heads * headdim
    steps = zx.shape[0] * chunks // rows
    tail = cx.shape[1]
    tokens = group * steps
    calls = rows // group // chunks
    offset = chunk * calls

    def step_block(*shape):
        return pl.BlockSpec(shape, lambda i, c: (i,) + (0,) * (len(shape) - 1))

    def pool_block(*shape):
        return pl.BlockSpec(shape, lambda i, c: (i + offset,) + (0,) * (len(shape) - 1))

    def whole(a):
        return pl.BlockSpec(a.shape, lambda i, c: (0,) * a.ndim)

    return pl.pallas_call(
        functools.partial(core_kernel, group, offset),
        grid_spec=pltpu.PrefetchScalarGridSpec(
            num_scalar_prefetch=1,
            grid=(calls,),
            in_specs=[
                step_block(tokens, 2 * chans),
                step_block(tokens, bcdt.shape[1]),
                pool_block(group, heads, headdim, nstate),
                pool_block(group, tail, chans),
                pool_block(group, tail, 2 * nstate),
                whole(cxw),
                whole(cbw),
                whole(head_params),
                whole(gain),
            ]
            + [pl.BlockSpec(memory_space=pl.ANY)] * len(done),
            out_specs=[
                step_block(tokens, chans),
                step_block(tokens, 1),
                pool_block(group, heads, headdim, nstate),
                pool_block(group, tail, chans),
                pool_block(group, tail, 2 * nstate),
            ],
            scratch_shapes=[
                pltpu.VMEM((group, 8 + steps, chans), f32),
                pltpu.VMEM((group, 8 + steps, 2 * nstate), f32),
            ],
        ),
        out_shape=[
            jax.ShapeDtypeStruct((zx.shape[0], chans), bf16),
            jax.ShapeDtypeStruct((zx.shape[0], 1), f32),
            jax.ShapeDtypeStruct(states.shape, f32),
            jax.ShapeDtypeStruct(cx.shape, f32),
            jax.ShapeDtypeStruct(cbc.shape, f32),
        ],
        input_output_aliases={10 + k: 2 + k for k in range(len(done))},
        compiler_params=pltpu.CompilerParams(vmem_limit_bytes=40 * 1024 * 1024),
        cost_estimate=pl.CostEstimate(
            flops=2 * zx.shape[0] * chans * nstate * 8,
            bytes_accessed=8 * (rows // chunks) * chans * nstate,
            transcendentals=zx.shape[0] * chans * 2,
        ),
        name="core",
    )(counted, zx, bcdt, states, cx, cbc, cxw, cbw, head_params, gain, *done)


def exchange_kernel(peers, per_peer, out_order, in_order, src, dst, outgoing, arrived, send_sem, recv_sem):
    me = lax.axis_index("req")
    rows = peers * per_peer
    barrier = pltpu.get_barrier_semaphore()
    for step in range(1, peers):
        pl.semaphore_signal(
            barrier, inc=1, device_id={"req": lax.rem(me + step, peers)}, device_id_type=pl.DeviceIdType.MESH
        )

    def gather(i, carry):
        outgoing[i] = src[out_order[i]]
        return carry

    lax.fori_loop(0, rows, gather, 0)
    pl.semaphore_wait(barrier, peers - 1)
    copies = []
    for step in range(1, peers):
        peer = lax.rem(me + step, peers)
        copy = pltpu.make_async_remote_copy(
            src_ref=outgoing.at[pl.ds(peer * per_peer, per_peer)],
            dst_ref=arrived.at[pl.ds(me * per_peer, per_peer)],
            send_sem=send_sem.at[step - 1],
            recv_sem=recv_sem.at[step - 1],
            device_id={"req": peer},
            device_id_type=pl.DeviceIdType.MESH,
        )
        copy.start()
        copies.append(copy)
    arrived[pl.ds(me * per_peer, per_peer)] = outgoing[pl.ds(me * per_peer, per_peer)]
    for copy in copies:
        copy.wait()

    def scatter(i, carry):
        dst[i] = arrived[in_order[i]]
        return carry

    lax.fori_loop(0, rows, scatter, 0)


def exchange(array, out_order, in_order, peers):
    per_peer = array.shape[0] // peers
    return pl.pallas_call(
        functools.partial(exchange_kernel, peers, per_peer),
        out_shape=jax.ShapeDtypeStruct(array.shape, array.dtype),
        in_specs=[pl.BlockSpec(memory_space=pltpu.SMEM)] * 2 + [pl.BlockSpec(memory_space=pltpu.VMEM)],
        out_specs=pl.BlockSpec(memory_space=pltpu.VMEM),
        scratch_shapes=[
            pltpu.VMEM(array.shape, array.dtype),
            pltpu.VMEM(array.shape, array.dtype),
            pltpu.SemaphoreType.DMA((peers - 1,)),
            pltpu.SemaphoreType.DMA((peers - 1,)),
        ],
        compiler_params=pltpu.CompilerParams(collective_id=0, has_side_effects=True),
        name="exchange",
    )(out_order, in_order, array)


def routes(slot, rows, myself, peers):
    per_peer = rows // peers
    blocks = slot.reshape(peers, rows)
    owner = blocks // rows
    earlier = jnp.arange(rows)[None, :, None] > jnp.arange(rows)[None, None, :]
    rank = jnp.sum((owner[:, :, None] == owner[:, None, :]) & earlier, axis=2, dtype=jnp.int32)
    places = jnp.arange(rows, dtype=jnp.int32)
    my_owner = lax.dynamic_index_in_dim(owner, myself, 0, keepdims=False)
    my_rank = lax.dynamic_index_in_dim(rank, myself, 0, keepdims=False)
    home = my_owner * per_peer + my_rank
    send_order = jnp.sum(jnp.where(home[None, :] == places[:, None], places[None, :], 0), axis=1, dtype=jnp.int32)
    arrive = (jnp.arange(peers, dtype=jnp.int32)[:, None] * per_peer + rank).reshape(-1)
    flat = slot.reshape(-1)
    hit = flat[None, :] == (myself * rows + places)[:, None]
    to_pool = jnp.sum(jnp.where(hit, arrive[None, :], 0), axis=1, dtype=jnp.int32)
    request = jnp.sum(jnp.where(hit, jnp.arange(flat.shape[0], dtype=jnp.int32)[None, :], 0), axis=1, dtype=jnp.int32)
    back_order = jnp.sum(jnp.where(to_pool[None, :] == places[:, None], places[None, :], 0), axis=1, dtype=jnp.int32)
    return send_order, to_pool, back_order, home, request


def per_device(
    hidden,
    w_zx,
    w_bc,
    w_dt,
    conv_x_w,
    conv_bc_w,
    dt_bias,
    a_log,
    d_skip,
    norm_gain,
    w_out,
    ssm_state,
    conv_x_state,
    conv_bc_state,
    slot,
    lengths,
    accepted,
):
    rows, steps, width_part = hidden.shape
    width = w_zx.shape[0]
    chans = w_zx.shape[2]
    myself = lax.axis_index("req")
    peers = lax.axis_size("req")
    send_order, to_pool, back_order, home, request = routes(slot, rows, myself, peers)
    counted = jnp.minimum(accepted, lengths)
    hit = jnp.arange(slot.shape[0], dtype=jnp.int32)[None, :] == request[:, None]
    my_counted = jnp.sum(jnp.where(hit, counted[None, :], 0), axis=1, dtype=jnp.int32)

    pooled = exchange(hidden, send_order, to_pool, peers)
    chunks = 2
    part = rows // chunks
    flat_zx = w_zx.reshape(width, 2 * chans)
    w_bcdt = jnp.concatenate([w_bc, w_dt], axis=1)
    head_params = jnp.stack([dt_bias, a_log, d_skip])
    hold = lax.optimization_barrier

    gathered = []
    for c in range(chunks):
        piece = pooled[c * part : (c + 1) * part]
        if c > 0:
            gathered[-1], piece, flat_zx = hold((gathered[-1], piece, flat_zx))
        gathered.append(lax.all_gather(piece, "head", axis=2, tiled=True))
    done, squares, summed = (), [], []
    for c in range(chunks):
        tokens = gathered[c].reshape(part * steps, width)
        zx = jnp.dot(tokens, flat_zx, preferred_element_type=f32).astype(bf16)
        bcdt = jnp.dot(tokens, w_bcdt, preferred_element_type=f32).astype(bf16)
        g, sq, *done = core(
            my_counted,
            zx,
            bcdt,
            ssm_state,
            conv_x_state,
            conv_bc_state,
            conv_x_w,
            conv_bc_w,
            head_params,
            norm_gain[None, :],
            4,
            c,
            chunks,
            done,
        )
        squares.append(sq)
        shares = jnp.dot(g, w_out, preferred_element_type=f32).astype(bf16)
        if c > 0:
            summed[-1], shares = hold((summed[-1], shares))
        summed.append(lax.psum_scatter(shares, "head", scatter_dimension=1, tiled=True))
    new_state, new_conv_x, new_conv_bc = done
    square = jnp.concatenate(squares, axis=0).reshape(-1, 128)
    total = jnp.sum(lax.all_gather(square, "head", axis=0), axis=0).reshape(rows * steps, 1)
    meansq = total / (chans * lax.axis_size("head"))
    full = jnp.concatenate(summed, axis=0).astype(f32)
    result = (full * lax.rsqrt(meansq + 1e-05)).astype(bf16).reshape(rows, steps, width_part)
    mine = exchange(result, back_order, home, peers)
    my_lengths = lax.dynamic_slice_in_dim(lengths, myself * rows, rows, 0)
    valid = jnp.arange(steps, dtype=jnp.int32)[None, :] < my_lengths[:, None]
    out = jnp.where(valid[..., None], mine, jnp.zeros((), bf16))
    return (out, new_state, new_conv_x, new_conv_bc)


def solution(mesh):
    in_specs = (
        P("req", None, "head"),
        P(None, None, "head"),
        P(),
        P(None, "head"),
        P(None, "head"),
        P(),
        P("head"),
        P("head"),
        P("head"),
        P("head"),
        P("head", None),
        P("req", "head", None, None),
        P("req", None, "head"),
        P("req", None, None),
        P(),
        P(),
        P(),
    )
    out_specs = (
        P("req", None, "head"),
        P("req", "head", None, None),
        P("req", None, "head"),
        P("req", None, None),
    )
    return jax.shard_map(
        per_device, mesh=mesh, in_specs=in_specs, out_specs=out_specs, check_vma=False
    )
```

```python
import functools

import jax
import jax.numpy as jnp
from jax import lax
from jax.experimental import pallas as pl
from jax.experimental.pallas import tpu as pltpu
from jax.sharding import PartitionSpec as P

highest = lax.Precision.HIGHEST
f32 = jnp.float32
bf16 = jnp.bfloat16


def iota(shape, dim):
    return lax.broadcasted_iota(jnp.int32, shape, dim)


def dot_nt(a, b):
    return lax.dot_general(a, b, (((1,), (1,)), ((), ())), preferred_element_type=f32)


def dot_nn(a, b, precision=None):
    return jnp.dot(a, b, preferred_element_type=f32, precision=precision)


def silu(v):
    return v * (1.0 / (1.0 + jnp.exp(-v)))


def conv(window_ref, prev_ref, inputs, taps, keep_ref, count_of, group, steps, tail):
    base = 8 - tail
    chans = inputs.shape[-1]
    window_ref[:, 0:8, :] = jnp.zeros((group, 8, inputs.shape[-1]), f32)
    window_ref[:, base:8, :] = prev_ref[...]
    window_ref[:, 8 : 8 + steps, :] = inputs.reshape(group, steps, chans)
    total = taps[tail + 1 : tail + 2, :][None]
    for tap in range(tail + 1):
        total = total + taps[tap : tap + 1, :][None] * window_ref[:, base + tap : base + tap + steps, :]
    for r in range(group):
        held = window_ref[r, :, :]
        place = iota((8 + steps, 1), 0) - base - count_of(r)
        for k in range(tail):
            keep_ref[r, k : k + 1, :] = jnp.sum(jnp.where(place == k, held, 0.0), axis=0, keepdims=True)
    return silu(total).astype(bf16).reshape(group * steps, chans)


def core_kernel(
    group,
    offset,
    counted_ref,
    zx_ref,
    bcdt_ref,
    state_ref,
    cx_ref,
    cbc_ref,
    cxw_ref,
    cbw_ref,
    heads_ref,
    gain_ref,
    *refs,
):
    (g_ref, sq_ref, new_state_ref, ncx_ref, ncbc_ref, xwin, bcwin) = refs[-7:]
    heads, headdim, nstate = state_ref.shape[1:]
    chans = heads * headdim
    tokens = zx_ref.shape[0]
    steps = tokens // group
    tail = cx_ref.shape[1]
    first = (pl.program_id(0) + offset) * group

    def count_of(r):
        return counted_ref[first + r]

    bcdt = bcdt_ref[...].astype(f32)
    x = conv(xwin, cx_ref, zx_ref[:, chans:].astype(f32), cxw_ref[...], ncx_ref, count_of, group, steps, tail)
    bc = conv(bcwin, cbc_ref, bcdt[:, : 2 * nstate], cbw_ref[...], ncbc_ref, count_of, group, steps, tail)
    bmat, cmat = bc[:, :nstate], bc[:, nstate:]
    xf = x.astype(f32)

    dt_bias, a_log, d_skip = heads_ref[0:1, :], heads_ref[1:2, :], heads_ref[2:3, :]
    raw = bcdt[:, 2 * nstate :] + dt_bias
    dt = jnp.maximum(raw, 0.0) + jnp.log1p(jnp.exp(-jnp.abs(raw)))
    rate = dt * -jnp.exp(a_log)

    row, col = iota((tokens, tokens), 0), iota((tokens, tokens), 1)
    same = row // steps == col // steps
    lower = jnp.where(same & (row >= col), 1.0, 0.0)
    cumul = dot_nn(lower, rate, highest)
    token = iota((tokens, heads), 0)
    limit = jnp.zeros((tokens, heads), jnp.int32)
    for r in range(group):
        limit = jnp.where(token // steps == r, count_of(r), limit)
    live = (token % steps) < limit
    total = dot_nn(jnp.where(same, 1.0, 0.0), jnp.where(live, rate, 0.0), highest)
    scaled = jnp.where(live, jnp.exp(jnp.where(live, total - cumul, 0.0)) * dt, 0.0)
    spread_to = jnp.where(iota((heads, chans), 1) // headdim == iota((heads, chans), 0), 1.0, 0.0).astype(bf16)
    dt_e = dot_nn(dt.astype(bf16), spread_to)
    scaled_e = dot_nn(scaled.astype(bf16), spread_to)
    carry_e = dot_nn(jnp.exp(cumul).astype(bf16), spread_to)
    skip_hi = d_skip.astype(bf16)
    skip_lo = (d_skip - skip_hi.astype(f32)).astype(bf16)
    skip_e = dot_nn(jnp.broadcast_to(skip_hi, (8, heads)), spread_to) + dot_nn(
        jnp.broadcast_to(skip_lo, (8, heads)), spread_to
    )
    mixed_skip = skip_e[0:1, :] * xf
    dtx = (dt_e * xf).astype(bf16)
    sxt = (scaled_e * xf).T.astype(bf16)
    btok = iota((tokens, nstate), 0) // steps
    bsel = jnp.concatenate([jnp.where(btok == r, bmat.astype(f32), 0.0) for r in range(group)], axis=1).astype(bf16)
    grown = dot_nn(sxt, bsel)

    wide = heads * steps
    spread_hs = jnp.where(iota((heads, wide), 1) // steps == iota((heads, wide), 0), 1.0, 0.0)
    cumul_hs = dot_nn(cumul, spread_hs, highest)
    t_at, s_at = iota((steps, wide), 0), iota((steps, wide), 1) % steps
    block = (iota((wide, chans), 0) // steps == iota((wide, chans), 1) // headdim).astype(f32).astype(bf16)
    eye = iota((heads, heads), 0) == iota((heads, heads), 1)

    pieces = []
    for r in range(group):
        span = slice(r * steps, (r + 1) * steps)
        c_r = cmat[span, :]
        b_r = bmat[span, :]
        inner = dot_nt(c_r, jnp.concatenate([b_r] * heads, axis=0))
        here = cumul_hs[span, :]
        there = jnp.sum(jnp.where(t_at == s_at, here, 0.0), axis=0, keepdims=True)
        factor = jnp.where(t_at >= s_at, jnp.exp(jnp.where(t_at >= s_at, here - there, 0.0)) * inner, 0.0)
        spreaded = jnp.concatenate([dtx[span, :]] * heads, axis=0) * block
        within = dot_nn(factor.astype(bf16), spreaded)
        states = state_ref[r].reshape(chans, nstate)
        carried = dot_nt(c_r, states.astype(bf16))
        pieces.append(carry_e[span, :] * carried + within)
        decay = jnp.sum(jnp.where(eye, jnp.exp(total[r * steps : r * steps + 1, :]), 0.0), axis=1, keepdims=True)
        for h in range(heads):
            new_state_ref[r, h] = (
                state_ref[r, h] * decay[h : h + 1, :]
                + grown[h * headdim : (h + 1) * headdim, r * nstate : (r + 1) * nstate]
            )
    mixed = (jnp.concatenate(pieces, axis=0) + mixed_skip).astype(bf16).astype(f32)
    gated = mixed * silu(zx_ref[:, :chans].astype(f32))
    sq_ref[...] = jnp.sum(gated * gated, axis=1, keepdims=True)
    g_ref[...] = (gated * gain_ref[...]).astype(bf16)


def core(counted, zx, bcdt, states, cx, cbc, cxw, cbw, head_params, gain, group, chunk, chunks, done):
    rows, heads, headdim, nstate = states.shape
    chans = heads * headdim
    steps = zx.shape[0] * chunks // rows
    tail = cx.shape[1]
    tokens = group * steps
    calls = rows // group // chunks
    offset = chunk * calls

    def step_block(*shape):
        return pl.BlockSpec(shape, lambda i, c: (i,) + (0,) * (len(shape) - 1))

    def pool_block(*shape):
        return pl.BlockSpec(shape, lambda i, c: (i + offset,) + (0,) * (len(shape) - 1))

    def whole(a):
        return pl.BlockSpec(a.shape, lambda i, c: (0,) * a.ndim)

    return pl.pallas_call(
        functools.partial(core_kernel, group, offset),
        grid_spec=pltpu.PrefetchScalarGridSpec(
            num_scalar_prefetch=1,
            grid=(calls,),
            in_specs=[
                step_block(tokens, 2 * chans),
                step_block(tokens, bcdt.shape[1]),
                pool_block(group, heads, headdim, nstate),
                pool_block(group, tail, chans),
                pool_block(group, tail, 2 * nstate),
                whole(cxw),
                whole(cbw),
                whole(head_params),
                whole(gain),
            ]
            + [pl.BlockSpec(memory_space=pl.ANY)] * len(done),
            out_specs=[
                step_block(tokens, chans),
                step_block(tokens, 1),
                pool_block(group, heads, headdim, nstate),
                pool_block(group, tail, chans),
                pool_block(group, tail, 2 * nstate),
            ],
            scratch_shapes=[
                pltpu.VMEM((group, 8 + steps, chans), f32),
                pltpu.VMEM((group, 8 + steps, 2 * nstate), f32),
            ],
        ),
        out_shape=[
            jax.ShapeDtypeStruct((zx.shape[0], chans), bf16),
            jax.ShapeDtypeStruct((zx.shape[0], 1), f32),
            jax.ShapeDtypeStruct(states.shape, f32),
            jax.ShapeDtypeStruct(cx.shape, f32),
            jax.ShapeDtypeStruct(cbc.shape, f32),
        ],
        input_output_aliases={10 + k: 2 + k for k in range(len(done))},
        compiler_params=pltpu.CompilerParams(vmem_limit_bytes=40 * 1024 * 1024),
        cost_estimate=pl.CostEstimate(
            flops=2 * zx.shape[0] * chans * nstate * 8,
            bytes_accessed=8 * (rows // chunks) * chans * nstate,
            transcendentals=zx.shape[0] * chans * 2,
        ),
        name="core",
    )(counted, zx, bcdt, states, cx, cbc, cxw, cbw, head_params, gain, *done)


def exchange_kernel(peers, per_peer, out_order, in_order, src, dst, outgoing, arrived, send_sem, recv_sem):
    me = lax.axis_index("req")
    rows = peers * per_peer
    barrier = pltpu.get_barrier_semaphore()
    for step in range(1, peers):
        pl.semaphore_signal(
            barrier, inc=1, device_id={"req": lax.rem(me + step, peers)}, device_id_type=pl.DeviceIdType.MESH
        )

    def gather(i, carry):
        outgoing[i] = src[out_order[i]]
        return carry

    lax.fori_loop(0, rows, gather, 0)
    pl.semaphore_wait(barrier, peers - 1)
    copies = []
    for step in range(1, peers):
        peer = lax.rem(me + step, peers)
        copy = pltpu.make_async_remote_copy(
            src_ref=outgoing.at[pl.ds(peer * per_peer, per_peer)],
            dst_ref=arrived.at[pl.ds(me * per_peer, per_peer)],
            send_sem=send_sem.at[step - 1],
            recv_sem=recv_sem.at[step - 1],
            device_id={"req": peer},
            device_id_type=pl.DeviceIdType.MESH,
        )
        copy.start()
        copies.append(copy)
    arrived[pl.ds(me * per_peer, per_peer)] = outgoing[pl.ds(me * per_peer, per_peer)]
    for copy in copies:
        copy.wait()

    def scatter(i, carry):
        dst[i] = arrived[in_order[i]]
        return carry

    lax.fori_loop(0, rows, scatter, 0)


def exchange(array, out_order, in_order, peers):
    per_peer = array.shape[0] // peers
    return pl.pallas_call(
        functools.partial(exchange_kernel, peers, per_peer),
        out_shape=jax.ShapeDtypeStruct(array.shape, array.dtype),
        in_specs=[pl.BlockSpec(memory_space=pltpu.SMEM)] * 2 + [pl.BlockSpec(memory_space=pltpu.VMEM)],
        out_specs=pl.BlockSpec(memory_space=pltpu.VMEM),
        scratch_shapes=[
            pltpu.VMEM(array.shape, array.dtype),
            pltpu.VMEM(array.shape, array.dtype),
            pltpu.SemaphoreType.DMA((peers - 1,)),
            pltpu.SemaphoreType.DMA((peers - 1,)),
        ],
        compiler_params=pltpu.CompilerParams(collective_id=0, has_side_effects=True),
        name="exchange",
    )(out_order, in_order, array)


def gather_head(piece):
    n = lax.axis_size("head")
    me = lax.axis_index("head")
    parts = [piece] + [lax.ppermute(piece, "head", [(i, (i + d) % n) for i in range(n)]) for d in range(1, n)]
    return jnp.concatenate([lax.select_n(lax.rem(me - j + n, n), *parts) for j in range(n)], axis=2)


def routes(slot, rows, myself, peers):
    per_peer = rows // peers
    blocks = slot.reshape(peers, rows)
    owner = blocks // rows
    earlier = jnp.arange(rows)[None, :, None] > jnp.arange(rows)[None, None, :]
    rank = jnp.sum((owner[:, :, None] == owner[:, None, :]) & earlier, axis=2, dtype=jnp.int32)
    places = jnp.arange(rows, dtype=jnp.int32)
    my_owner = lax.dynamic_index_in_dim(owner, myself, 0, keepdims=False)
    my_rank = lax.dynamic_index_in_dim(rank, myself, 0, keepdims=False)
    home = my_owner * per_peer + my_rank
    send_order = jnp.sum(jnp.where(home[None, :] == places[:, None], places[None, :], 0), axis=1, dtype=jnp.int32)
    arrive = (jnp.arange(peers, dtype=jnp.int32)[:, None] * per_peer + rank).reshape(-1)
    flat = slot.reshape(-1)
    hit = flat[None, :] == (myself * rows + places)[:, None]
    to_pool = jnp.sum(jnp.where(hit, arrive[None, :], 0), axis=1, dtype=jnp.int32)
    request = jnp.sum(jnp.where(hit, jnp.arange(flat.shape[0], dtype=jnp.int32)[None, :], 0), axis=1, dtype=jnp.int32)
    back_order = jnp.sum(jnp.where(to_pool[None, :] == places[:, None], places[None, :], 0), axis=1, dtype=jnp.int32)
    return send_order, to_pool, back_order, home, request


def per_device(
    hidden,
    w_zx,
    w_bc,
    w_dt,
    conv_x_w,
    conv_bc_w,
    dt_bias,
    a_log,
    d_skip,
    norm_gain,
    w_out,
    ssm_state,
    conv_x_state,
    conv_bc_state,
    slot,
    lengths,
    accepted,
):
    rows, steps, width_part = hidden.shape
    width = w_zx.shape[0]
    chans = w_zx.shape[2]
    myself = lax.axis_index("req")
    peers = lax.axis_size("req")
    send_order, to_pool, back_order, home, request = routes(slot, rows, myself, peers)
    counted = jnp.minimum(accepted, lengths)
    hit = jnp.arange(slot.shape[0], dtype=jnp.int32)[None, :] == request[:, None]
    my_counted = jnp.sum(jnp.where(hit, counted[None, :], 0), axis=1, dtype=jnp.int32)

    pooled = exchange(hidden, send_order, to_pool, peers)
    chunks = 2
    part = rows // chunks
    flat_zx = w_zx.reshape(width, 2 * chans)
    w_bcdt = jnp.concatenate([w_bc, w_dt], axis=1)
    head_params = jnp.stack([dt_bias, a_log, d_skip])
    hold = lax.optimization_barrier

    gathered = []
    for c in range(chunks):
        piece = pooled[c * part : (c + 1) * part]
        if c > 0:
            gathered[-1], piece, flat_zx = hold((gathered[-1], piece, flat_zx))
        gathered.append(gather_head(piece))
    done, squares, summed = (), [], []
    for c in range(chunks):
        tokens = gathered[c].reshape(part * steps, width)
        zx = jnp.dot(tokens, flat_zx, preferred_element_type=f32).astype(bf16)
        bcdt = jnp.dot(tokens, w_bcdt, preferred_element_type=f32).astype(bf16)
        g, sq, *done = core(
            my_counted,
            zx,
            bcdt,
            ssm_state,
            conv_x_state,
            conv_bc_state,
            conv_x_w,
            conv_bc_w,
            head_params,
            norm_gain[None, :],
            4,
            c,
            chunks,
            done,
        )
        squares.append(sq)
        shares = jnp.dot(g, w_out, preferred_element_type=f32).astype(bf16)
        if c > 0:
            summed[-1], shares = hold((summed[-1], shares))
        summed.append(lax.psum_scatter(shares, "head", scatter_dimension=1, tiled=True))
    new_state, new_conv_x, new_conv_bc = done
    square = jnp.concatenate(squares, axis=0).reshape(-1, 128)
    total = jnp.sum(lax.all_gather(square, "head", axis=0), axis=0).reshape(rows * steps, 1)
    meansq = total / (chans * lax.axis_size("head"))
    full = jnp.concatenate(summed, axis=0).astype(f32)
    result = (full * lax.rsqrt(meansq + 1e-05)).astype(bf16).reshape(rows, steps, width_part)
    mine = exchange(result, back_order, home, peers)
    my_lengths = lax.dynamic_slice_in_dim(lengths, myself * rows, rows, 0)
    valid = jnp.arange(steps, dtype=jnp.int32)[None, :] < my_lengths[:, None]
    out = jnp.where(valid[..., None], mine, jnp.zeros((), bf16))
    return (out, new_state, new_conv_x, new_conv_bc)


def solution(mesh):
    in_specs = (
        P("req", None, "head"),
        P(None, None, "head"),
        P(),
        P(None, "head"),
        P(None, "head"),
        P(),
        P("head"),
        P("head"),
        P("head"),
        P("head"),
        P("head", None),
        P("req", "head", None, None),
        P("req", None, "head"),
        P("req", None, None),
        P(),
        P(),
        P(),
    )
    out_specs = (
        P("req", None, "head"),
        P("req", "head", None, None),
        P("req", None, "head"),
        P("req", None, None),
    )
    return jax.shard_map(
        per_device, mesh=mesh, in_specs=in_specs, out_specs=out_specs, check_vma=False
    )
```
